512 devices in a mesh: section: 8 (over y), dom: 64 (over z, x, core).
Axes of the slice: x: 4, y: 8, z: 8, core: 2. Of those that a mesh axis runs over, the one named last changes fastest.
Arguments:
- node_states: bfloat16 [8, 1, 12288, 512], P('section', None, 'dom'), may hold values from -6 to 6
- edge_features: bfloat16 [1, 24576, 512], P(None, 'dom'), may hold values from -6 to 6
- out_cotangent: bfloat16 [1, 12288, 512], P(None, 'dom'), may hold values from -6 to 6
- edge_weight: bfloat16 [8, 512, 512], P('section'), may hold values from -0.25 to 0.25
- send_weight: bfloat16 [8, 512, 512], P('section'), may hold values from -0.25 to 0.25
- layer_norm_gain: float32 [8, 512], P('section'), may hold values from 0.5 to 1.5
- edge_sender: int32 [24576], P('dom'), may hold values from 0 to 255
- edge_receiver: int32 [24576], P('dom'), may hold values from 0 to 191
- halo_rows: int32 [4096], P('dom'), may hold values from 0 to 191
- block_counts: int32 [64], P('dom'), may hold values from 1 to 3, as said below
Outputs:
- node_grads: bfloat16 [8, 1, 12288, 512], P('section', None, 'dom')
- edge_grads: bfloat16 [1, 24576, 512], P(None, ('dom', 'section'))
- edge_weight_grad: float32 [8, 512, 512], P('section', 'dom')
- send_weight_grad: float32 [8, 512, 512], P('section', 'dom')
- gain_grad: float32 [8, 512], P('section', 'dom')
The draws below stay inside these ranges and needn't reach their ends.
Inputs may be any that keep to these rules, and one draw needn't show every extreme that they name: `block_counts`: every partition has at least one live block and some partition has all 3 blocks live.
All inputs are finite; a program needn't handle non-finite values.
Results may differ from the reference program's by a relative error of at most 0.028.
Values may be sent and summed in bfloat16 or wider, within the bound.
No kernel may reach another device: no remote copies, remote signals or barrier semaphores. Data moves between devices by JAX's collectives and lax.ppermute only.
A program may use at most 64 MiB of HBM per device.

```python
import jax
import jax.numpy as jnp
from jax import lax

D = 512
N_DEV = 192
E_DEV = 384
SAMPLES = 1
HALO = 32
EDGE_BLOCK = 128
LAYERS = 8
PARTS_SIZE = 64
NODES = 12288
EDGES = 24576


def draw_block_counts(key, part):
    key = jax.random.fold_in(key, 11)
    first, second = jax.random.split(key)
    counts = jax.random.randint(first, (PARTS_SIZE,), 1, E_DEV // EDGE_BLOCK + 1)
    chosen = jax.random.randint(second, (), 0, PARTS_SIZE)
    return jnp.where(jnp.arange(PARTS_SIZE) == chosen, E_DEV // EDGE_BLOCK, counts).astype(jnp.int32)


def touch_ends(array, own_key, smallest, largest):
    extent = array.shape
    index_at = [jax.random.randint(jax.random.fold_in(own_key, axis), (), 0, extent[axis]) for axis in range(len(extent))]
    array = array.at[tuple(index_at)].set(smallest)
    longest = extent.index(max(extent))
    index_at[longest] = (index_at[longest] + 1) % extent[longest]
    return array.at[tuple(index_at)].set(largest)


def block_levels(own_key, dims, shards, smallest, high):
    def one(dim, shards_of):
        steps = jax.random.uniform(jax.random.fold_in(jax.random.fold_in(own_key, 6), dim), (shards_of,), jnp.float32, smallest / len(shards), high / len(shards))
        return jnp.repeat(jnp.exp(steps), dims[dim] // shards_of).reshape((-1,) + (1,) * (len(dims) - dim - 1))

    factor_of = one(*shards[0])
    for cut in shards[1:]:
        factor_of = factor_of * one(*cut)
    return factor_of


def bell_draw(own_key, dims, width, limit, shards=(), kind=jnp.bfloat16):
    level = block_levels(own_key, dims, shards, -0.22, 0.18) if shards else 1.0
    values = jax.random.normal(own_key, dims, jnp.float32) * width * level
    return jnp.minimum(jnp.maximum(values, -limit), limit).astype(kind)


def setup_inputs(seed: int = 0) -> dict:
    splits = jax.random.split(jax.random.key(seed), 11)
    node_states = bell_draw(splits[0], (LAYERS, SAMPLES, NODES, D), 1.0, 6.0, ((0, 8), (2, 64)))
    edge_features = bell_draw(splits[1], (SAMPLES, EDGES, D), 1.0, 6.0, ((1, 64),))
    out_cotangent = bell_draw(splits[2], (SAMPLES, NODES, D), 1.0, 6.0, ((1, 64),))
    edge_weight = bell_draw(splits[3], (LAYERS, D, D), D ** -0.5, 0.25, ((0, 8),))
    send_weight = bell_draw(splits[4], (LAYERS, D, D), D ** -0.5, 0.25, ((0, 8),))
    layer_norm_gain = jnp.clip(1.0 + 0.1 * jax.random.normal(splits[5], (LAYERS, D), jnp.float32), 0.5, 1.5)
    edge_sender = touch_ends(jax.random.randint(splits[6], (EDGES,), 0, N_DEV + 2 * HALO), jax.random.fold_in(splits[6], 1), 0, (N_DEV + 2 * HALO) - 1).astype(jnp.int32)
    edge_receiver = touch_ends(jax.random.randint(splits[7], (EDGES,), 0, N_DEV), jax.random.fold_in(splits[7], 1), 0, N_DEV - 1).astype(jnp.int32)
    halo_rows = touch_ends(jax.random.randint(splits[8], (PARTS_SIZE * 2 * HALO,), 0, N_DEV), jax.random.fold_in(splits[8], 1), 0, N_DEV - 1).astype(jnp.int32)
    block_counts = draw_block_counts(jax.random.fold_in(splits[10], 71), 0)
    return {"node_states": node_states, "edge_features": edge_features, "out_cotangent": out_cotangent, "edge_weight": edge_weight, "send_weight": send_weight, "layer_norm_gain": layer_norm_gain, "edge_sender": edge_sender, "edge_receiver": edge_receiver, "halo_rows": halo_rows, "block_counts": block_counts}


NORM_EPSILON = 1e-05

def silu_slope(value):
    sig = jax.nn.sigmoid(value)
    return sig * (1.0 + value * (1.0 - sig))

def round_trip(value):
    return lax.optimization_barrier(value.astype(jnp.bfloat16)).astype(jnp.float32)

def reference(node_states, edge_features, out_cotangent, edge_weight, send_weight, layer_norm_gain, edge_sender, edge_receiver, halo_rows, block_counts):
    table_rows = N_DEV + 2 * HALO
    nodes_all = N_DEV * PARTS_SIZE
    edges_all = E_DEV * PARTS_SIZE
    position = jnp.arange(edges_all, dtype=jnp.int32)
    owner = position // E_DEV
    lower = (owner + PARTS_SIZE - 1) % PARTS_SIZE
    upper = (owner + 1) % PARTS_SIZE
    local = edge_sender
    from_lower = jnp.clip(local - N_DEV, 0, HALO - 1)
    from_upper = jnp.clip(local - N_DEV - HALO, 0, HALO - 1)
    lower_node = lower * N_DEV + halo_rows[lower * 2 * HALO + HALO + from_lower]
    upper_node = upper * N_DEV + halo_rows[upper * 2 * HALO + from_upper]
    global_sender = jnp.where(local < N_DEV, owner * N_DEV + local, jnp.where(local < N_DEV + HALO, lower_node, upper_node))
    global_receiver = owner * N_DEV + edge_receiver
    table_index = owner * table_rows + local
    live = (position % E_DEV // EDGE_BLOCK < block_counts[owner]).astype(jnp.float32)[None, :, None]
    parts = jnp.arange(PARTS_SIZE, dtype=jnp.int32)
    slot = jnp.arange(HALO, dtype=jnp.int32)
    lower_part = (parts + PARTS_SIZE - 1) % PARTS_SIZE
    upper_part = (parts + 1) % PARTS_SIZE
    lower_target = lower_part[:, None] * N_DEV + halo_rows[lower_part[:, None] * 2 * HALO + HALO + slot[None, :]]
    upper_target = upper_part[:, None] * N_DEV + halo_rows[upper_part[:, None] * 2 * HALO + slot[None, :]]
    halo_target = jnp.concatenate([lower_target, upper_target], axis=1).reshape(-1)
    flat_features = edge_features.reshape(-1, D)
    upstream = out_cotangent
    edge_total = jnp.zeros((SAMPLES, edges_all, D), jnp.float32)
    node_list, edge_list, send_list, gain_list = ([], [], [], [])
    for layer in range(LAYERS - 1, -1, -1):
        states = node_states[layer]
        w_edge = edge_weight[layer]
        sender_weight = send_weight[layer]
        gain = layer_norm_gain[layer].astype(jnp.float32)
        projected_features = jnp.dot(states, sender_weight, preferred_element_type=jnp.float32).astype(jnp.bfloat16)
        pre = jnp.dot(edge_features, w_edge, preferred_element_type=jnp.float32) + projected_features[:, global_sender].astype(jnp.float32)
        message = (live * jax.nn.silu(pre)).astype(jnp.bfloat16)
        summed = jax.ops.segment_sum(jnp.moveaxis(message.astype(jnp.float32), 1, 0), global_receiver, num_segments=nodes_all)
        agg = jnp.moveaxis(summed, 0, 1)
        scale = lax.rsqrt(lax.optimization_barrier(jnp.mean(agg * agg, axis=-1, keepdims=True)) + NORM_EPSILON)
        normed = agg * scale
        up_wide = upstream.astype(jnp.float32)
        gain_list.append(lax.optimization_barrier(jnp.sum(up_wide * normed, axis=(0, 1))))
        dnorm = up_wide * gain
        dagg = (scale * (dnorm - normed * lax.optimization_barrier(jnp.mean(dnorm * normed, axis=-1, keepdims=True)))).astype(jnp.bfloat16)
        dpre = (live * dagg[:, global_receiver].astype(jnp.float32) * silu_slope(pre)).astype(jnp.bfloat16)
        edge_total = edge_total + round_trip(jnp.dot(dpre, w_edge.T, preferred_element_type=jnp.float32))
        edge_list.append(jnp.dot(flat_features.T, dpre.reshape(-1, D), preferred_element_type=jnp.float32))
        table_grad = jax.ops.segment_sum(jnp.moveaxis(dpre.astype(jnp.float32), 1, 0), table_index, num_segments=PARTS_SIZE * table_rows)
        table_grad = table_grad.reshape(PARTS_SIZE, table_rows, SAMPLES, D)
        own = table_grad[:, :N_DEV].reshape(nodes_all, SAMPLES, D)
        halo_part = round_trip(table_grad[:, N_DEV:]).reshape(PARTS_SIZE * 2 * HALO, SAMPLES, D)
        returned = jax.ops.segment_sum(halo_part, halo_target, num_segments=nodes_all)
        dproj = jnp.moveaxis(own + returned, 1, 0).astype(jnp.bfloat16)
        send_list.append(jnp.dot(states.reshape(-1, D).T, dproj.reshape(-1, D), preferred_element_type=jnp.float32))
        upstream = (up_wide + jnp.dot(dproj, sender_weight.T, preferred_element_type=jnp.float32)).astype(jnp.bfloat16)
        node_list.append(upstream)
    node_grads = jnp.stack(node_list[::-1])
    edge_grads = edge_total.astype(jnp.bfloat16)
    return (node_grads, edge_grads, jnp.stack(edge_list[::-1]), jnp.stack(send_list[::-1]), jnp.stack(gain_list[::-1]))
```

```python
import numpy as np
import jax
import jax.numpy as jnp
from jax import lax
from jax.sharding import PartitionSpec as P

EDGE_BLOCK = 128
NORM_EPSILON = 1e-05

GRAY = {2: (0, 1), 4: (0, 1, 3, 2), 8: (0, 1, 3, 2, 6, 7, 5, 4)}

STEPS = {
    0: (("c", 0), ("x", 0), ("z", 0), ("x", 1), ("z", 1), ("z", 2)),
    1: (("c", 0), ("z", 0), ("x", 0), ("z", 1), ("x", 1), ("z", 2)),
}


def coordinates(p):
    return {"z": p // 8, "x": (p // 2) % 4, "c": p % 2}


def index_of(at):
    return at["z"] * 8 + at["x"] * 2 + at["c"]


SIZES = {"z": 8, "x": 4, "c": 2}


def flipped(p, step):
    axis, bit = step
    at = dict(coordinates(p))
    gray = GRAY[SIZES[axis]]
    at[axis] = gray.index(gray[at[axis]] ^ (1 << bit))
    return index_of(at)


def dom_partner(p, k):
    return flipped(p, STEPS[p % 2][k])


def dom_order():
    table = np.zeros((64, 64), np.int32)
    for p in range(64):
        for j in range(64):
            q = p
            core = (p % 2) ^ (j >> 5)
            for k in range(6):
                if (j >> (5 - k)) & 1:
                    q = flipped(q, STEPS[core][k])
            table[p, j] = q
    return table


def section_flip(s, bit):
    gray = GRAY[8]
    return gray.index(gray[s] ^ (1 << bit))


def section_order():
    table = np.zeros((8, 8), np.int32)
    for s in range(8):
        for j in range(8):
            q = s
            for k in range(3):
                if (j >> (2 - k)) & 1:
                    q = section_flip(q, k)
            table[s, j] = q
    return table


def onehot(index, count):
    return (index[:, None] == jnp.arange(count, dtype=jnp.int32)[None, :]).astype(jnp.bfloat16)


def onehot_t(index, count):
    return (jnp.arange(count, dtype=jnp.int32)[:, None] == index[None, :]).astype(jnp.bfloat16)


def dot(a, b):
    return jnp.dot(a, b, preferred_element_type=jnp.float32)


def dot_t(a, b):
    return lax.dot_general(a, b, (((1,), (1,)), ((), ())), preferred_element_type=jnp.float32)


def spread(chunks, size):
    return (chunks[:, None] * size + jnp.arange(size, dtype=jnp.int32)[None, :]).reshape(-1)


def on_device(
    node_states,
    edge_features,
    out_cotangent,
    edge_weight,
    send_weight,
    layer_norm_gain,
    edge_sender,
    edge_receiver,
    halo_rows,
    block_counts,
):
    bf16, f32 = jnp.bfloat16, jnp.float32
    h = node_states[0, 0]
    feats = edge_features[0]
    w_edge, w_send, gain = edge_weight[0], send_weight[0], layer_norm_gain[0]
    nodes, width = h.shape
    edges = feats.shape[0]
    rim = halo_rows.shape[0] // 2
    rows = nodes + 2 * rim
    sections, doms = lax.axis_size("section"), lax.axis_size("dom")
    section, dom = lax.axis_index("section"), lax.axis_index("dom")

    up_pairs = [(p, (p + 1) % doms) for p in range(doms)]
    down_pairs = [(p, (p - 1) % doms) for p in range(doms)]

    select = onehot(halo_rows, nodes)
    select_t = onehot_t(halo_rows, nodes)
    chosen = dot(select, h).astype(bf16)
    from_low = lax.ppermute(chosen[rim:], "dom", up_pairs)
    from_high = lax.ppermute(chosen[:rim], "dom", down_pairs)
    h_rim = jnp.concatenate([from_low, from_high], axis=0)
    send_hot = onehot(edge_sender, rows)
    send_hot_t = onehot_t(edge_sender, rows)
    recv_hot = onehot(edge_receiver, nodes)
    recv_hot_t = onehot_t(edge_receiver, nodes)
    live = (jnp.arange(edges, dtype=jnp.int32) // EDGE_BLOCK < block_counts[0]).astype(f32)[:, None]
    own = dot(h, w_send).astype(bf16)
    pre = dot(feats, w_edge) + dot(send_hot[:, :nodes], own)
    pre = pre + dot(send_hot[:, nodes:], dot(h_rim, w_send).astype(bf16))
    sig = jax.nn.sigmoid(pre)
    message = (live * (pre * sig)).astype(bf16)
    slope = live * (sig * (1.0 + pre * (1.0 - sig)))
    agg = dot(recv_hot_t, message)
    scale = lax.rsqrt(jnp.mean(agg * agg, axis=-1, keepdims=True) + NORM_EPSILON)
    normed = agg * scale

    def backward(up):
        up_wide = up.astype(f32)
        dnorm = up_wide * gain
        dagg = scale * (dnorm - normed * jnp.mean(dnorm * normed, axis=-1, keepdims=True))
        gathered = dot(recv_hot, dagg.astype(bf16))
        dpre = (slope * gathered).astype(bf16)
        return dpre, dot(send_hot_t, dpre).astype(bf16)

    def parts(up, table):
        back = dot_t(table, w_send)
        return (up.astype(f32) + back[:nodes]).astype(bf16), back[nodes:].astype(bf16)

    def joined(part, rims):
        return (part.astype(f32) + dot(select_t, rims)).astype(bf16)

    def hop(value, t, shift):
        top = sections - 1 - t
        pairs = [(top * doms + p, (top - 1) * doms + (p + shift) % doms) for p in range(doms)]
        return lax.ppermute(value, ("section", "dom"), pairs)

    up = out_cotangent[0]
    held = jnp.where(section == sections - 1, up, jnp.zeros_like(up))
    held_rims = jnp.zeros((2 * rim, width), bf16)
    for t in range(sections - 1):
        _, table = backward(up)
        part, edge_rows = parts(up, table)
        part = hop(part, t, 0)
        rims = jnp.concatenate([hop(edge_rows[rim:], t, 1), hop(edge_rows[:rim], t, -1)], axis=0)
        up = joined(part, rims)
        if t < sections - 2:
            held, held_rims = held + part, held_rims + rims

    held, held_rims = lax.optimization_barrier((held, held_rims))
    up = joined(held + part, held_rims + rims)

    order = lax.dynamic_index_in_dim(jnp.asarray(dom_order()), dom, 0, keepdims=False)
    mixer = onehot(spread(order, width // doms), width)
    feats_t = dot_t(mixer, feats).astype(bf16)
    h_t = jnp.concatenate([dot_t(mixer, h), dot_t(mixer, h_rim)], axis=1).astype(bf16)
    half = width // 2

    dpre, table = backward(up)
    gain_part = jnp.sum(up.astype(f32) * normed, axis=0)

    def gain_rows(total):
        high = total.astype(bf16)
        low = (total - high.astype(f32)).astype(bf16)
        return jnp.concatenate([high[None], low[None], jnp.zeros((6, width), bf16)], axis=0)

    edge_keep, send_keep = dot(feats_t[:half], dpre), dot(h_t[:half], table)
    edge_send, send_send = dot(feats_t[half:], dpre), dot(h_t[half:], table)
    keep = jnp.concatenate([edge_keep, send_keep], axis=0)
    away = jnp.concatenate([edge_send, send_send], axis=0).astype(bf16)
    total = gain_part
    size = half
    for k in range(6):
        pairs = [(p, dom_partner(p, k)) for p in range(doms)]
        got = lax.ppermute(jnp.concatenate([away, gain_rows(total)], axis=0), "dom", pairs)
        keep = keep + got[: 2 * size].astype(f32)
        total = total + got[2 * size].astype(f32) + got[2 * size + 1].astype(f32)
        if k < 5:
            size = size // 2
            away = jnp.concatenate([keep[size : 2 * size], keep[3 * size :]], axis=0).astype(bf16)
            keep = jnp.concatenate([keep[:size], keep[2 * size : 3 * size]], axis=0)
    edge_grad, send_grad = keep[:size], keep[size:]
    gain_grad = lax.dynamic_slice_in_dim(total, dom * size, size, 0)

    part, edge_rows = parts(up, table)
    rims = jnp.concatenate(
        [
            lax.ppermute(edge_rows[rim:], "dom", up_pairs),
            lax.ppermute(edge_rows[:rim], "dom", down_pairs),
        ],
        axis=0,
    )
    node_grads = joined(part, rims)

    s_order = lax.dynamic_index_in_dim(jnp.asarray(section_order()), section, 0, keepdims=False)
    s_mixer = onehot(spread(s_order, edges // sections), edges)
    term = dot_t(dot(s_mixer, dpre).astype(bf16), w_edge).astype(bf16)
    for k in range(3):
        pairs = [(s, section_flip(s, k)) for s in range(sections)]
        middle = term.shape[0] // 2
        got = lax.ppermute(term[middle:], "section", pairs)
        term = (term[:middle].astype(f32) + got.astype(f32)).astype(bf16)

    return (
        node_grads[None, None],
        term[None],
        edge_grad[None],
        send_grad[None],
        gain_grad[None],
    )


def solution(mesh):
    return jax.shard_map(
        on_device,
        mesh=mesh,
        in_specs=(
            P("section", None, "dom", None),
            P(None, "dom", None),
            P(None, "dom", None),
            P("section", None, None),
            P("section", None, None),
            P("section", None),
            P("dom"),
            P("dom"),
            P("dom"),
            P("dom"),
        ),
        out_specs=(
            P("section", None, "dom", None),
            P(None, ("dom", "section"), None),
            P("section", "dom", None),
            P("section", "dom", None),
            P("section", "dom"),
        ),
        check_vma=False,
    )
```

```python
import numpy as np
import jax
import jax.numpy as jnp
from jax import lax
from jax.sharding import PartitionSpec as P

EDGE_BLOCK = 128
NORM_EPSILON = 1e-05

ALONG_X = [[z * 8 + x * 2 + c for x in range(4)] for z in range(8) for c in range(2)]
ALONG_Z = [[z * 8 + x * 2 + c for z in range(8)] for x in range(4) for c in range(2)]


def section_order(sections):
    table = np.zeros((sections, sections), np.int32)
    for s in range(sections):
        for j in range(sections):
            table[s, j] = s ^ sum(((j >> (2 - k)) & 1) << k for k in range(3))
    return table


def after(mark, *values):
    return lax.optimization_barrier((mark, *values))[1:]


def onehot(index, count):
    return (index[:, None] == jnp.arange(count, dtype=jnp.int32)[None, :]).astype(jnp.bfloat16)


def onehot_t(index, count):
    return (jnp.arange(count, dtype=jnp.int32)[:, None] == index[None, :]).astype(jnp.bfloat16)


def dot(a, b):
    return jnp.dot(a, b, preferred_element_type=jnp.float32)


def dot_t(a, b):
    return lax.dot_general(a, b, (((1,), (1,)), ((), ())), preferred_element_type=jnp.float32)


def spread(chunks, size):
    return (chunks[:, None] * size + jnp.arange(size, dtype=jnp.int32)[None, :]).reshape(-1)


def on_device(
    node_states,
    edge_features,
    out_cotangent,
    edge_weight,
    send_weight,
    layer_norm_gain,
    edge_sender,
    edge_receiver,
    halo_rows,
    block_counts,
):
    bf16, f32 = jnp.bfloat16, jnp.float32
    h = node_states[0, 0]
    feats = edge_features[0]
    w_edge, w_send, gain = edge_weight[0], send_weight[0], layer_norm_gain[0]
    nodes, width = h.shape
    edges = feats.shape[0]
    rim = halo_rows.shape[0] // 2
    rows = nodes + 2 * rim
    sections, doms = lax.axis_size("section"), lax.axis_size("dom")
    section, dom = lax.axis_index("section"), lax.axis_index("dom")

    near = [p ^ 1 for p in range(doms)]
    far = [(p + 1) % doms if p % 2 else (p - 1) % doms for p in range(doms)]
    near_pairs, far_pairs = list(enumerate(near)), list(enumerate(far))
    even = dom % 2 == 0
    label = jnp.arange(rows, dtype=jnp.int32)
    label = jnp.where(even & (label >= nodes), nodes + (label - nodes + rim) % (2 * rim), label)

    picks = jnp.concatenate([halo_rows, jnp.arange(nodes, dtype=jnp.int32)])
    chosen = lax.optimization_barrier(dot(onehot(picks, nodes), h).astype(bf16))
    from_far = lax.ppermute(jnp.where(even, chosen[:rim], chosen[rim : 2 * rim]), "dom", far_pairs)
    from_near = lax.ppermute(jnp.where(even, chosen[rim : 2 * rim], chosen[:rim]), "dom", near_pairs)
    h_rim = jnp.concatenate([from_near, from_far], axis=0)
    send_hot = (edge_sender[:, None] == label[None, :]).astype(bf16)
    send_hot_t = (label[:, None] == edge_sender[None, :]).astype(bf16)
    recv_hot = onehot(edge_receiver, nodes)
    recv_hot_t = onehot_t(edge_receiver, nodes)
    live = (jnp.arange(edges, dtype=jnp.int32) // EDGE_BLOCK < block_counts[0]).astype(f32)[:, None]
    own = dot(chosen[2 * rim :], w_send).astype(bf16)
    base = lax.optimization_barrier(dot(feats, w_edge) + dot(send_hot[:, :nodes], own))
    pre = lax.optimization_barrier(base + dot(send_hot[:, nodes:], dot(h_rim, w_send).astype(bf16)))
    sig = jax.nn.sigmoid(pre)
    message = (live * (pre * sig)).astype(bf16)
    slope = live * (sig * (1.0 + pre * (1.0 - sig)))
    slope = lax.optimization_barrier(slope)
    agg = dot(recv_hot_t, message)
    scale = lax.rsqrt(jnp.mean(agg * agg, axis=-1, keepdims=True) + NORM_EPSILON)
    normed = agg * scale

    def backward(up):
        up_wide = up.astype(f32)
        dnorm = up_wide * gain
        dagg = scale * (dnorm - normed * jnp.mean(dnorm * normed, axis=-1, keepdims=True))
        gathered = dot(recv_hot, dagg.astype(bf16))
        dpre = (slope * gathered).astype(bf16)
        return dpre, dot(send_hot_t, dpre).astype(bf16)

    def own_part(up, table):
        return (up.astype(f32) + dot_t(table[:nodes], w_send)).astype(bf16)

    def rim_part(table):
        return dot_t(table[nodes:], w_send).astype(bf16)

    def joined(part, from_near, from_far):
        (from_far,) = after(part, from_far)
        total = lax.optimization_barrier(part.astype(f32) + dot(far_t, from_far))
        (from_near,) = after(total, from_near)
        return (total + dot(near_t, from_near)).astype(bf16)

    def hop(value, t, target):
        top = sections - 1 - t
        pairs = [(top * doms + p, (top - 1) * doms + target[p]) for p in range(doms)]
        return lax.ppermute(value, ("section", "dom"), pairs)

    up = out_cotangent[0]
    held = jnp.where(section == sections - 1, up, jnp.zeros_like(up))
    for t in range(sections - 1):
        _, table = backward(up)
        rims = rim_part(table)
        part = own_part(up, table)
        if t == 0:
            (rows_late,) = after(part, halo_rows)
            near_t = onehot_t(jnp.where(even, rows_late[rim:], rows_late[:rim]), nodes)
            far_t = onehot_t(jnp.where(even, rows_late[:rim], rows_late[rim:]), nodes)
        from_far = hop(rims[rim:], t, far)
        from_near = hop(rims[:rim], t, near)
        up = joined(hop(part, t, range(doms)), from_near, from_far)
        if t == sections - 3:
            feats_late, h_late, h_rim_late, dom_late, section_late = after(part, feats, h, h_rim, dom, section)
            place = jnp.arange(doms, dtype=jnp.int32)
            chunk = (place % 8) * 8 + (place // 8 % 4) * 2 + (dom_late + place // 32) % 2
            mixer = onehot(spread(chunk, width // doms), width)
            feats_t = dot_t(mixer, feats_late).astype(bf16)
            h_t = jnp.concatenate([dot_t(mixer, h_late), dot_t(mixer, h_rim_late)], axis=1).astype(bf16)
            s_order = lax.dynamic_index_in_dim(jnp.asarray(section_order(sections)), section_late, 0, keepdims=False)
            s_order = spread(s_order, edges // sections)
            up, mixer, feats_t, h_t, s_order = lax.optimization_barrier((up, mixer, feats_t, h_t, s_order))
        if t < sections - 2:
            held = held + up
            held, up = lax.optimization_barrier((held, up))

    up = held + up
    dpre, table = backward(up)
    gain_part = jnp.sum(up.astype(f32) * normed, axis=0)

    def section_send(term, k):
        pairs = [(s, s ^ (1 << k)) for s in range(sections)]
        return lax.ppermute(term[term.shape[0] // 2 :], "section", pairs)

    def section_add(term, got):
        return (term[: term.shape[0] // 2].astype(f32) + got.astype(f32)).astype(bf16)

    half = width // 2
    gain_rows = jnp.broadcast_to(gain_part.astype(bf16)[None], (128, width))

    def gradients(at):
        return jnp.concatenate([dot(feats_t[at], dpre), dot(h_t[at], table), dot_t(mixer[at], gain_rows)], axis=1)

    rims = rim_part(table)
    beside = jnp.pad(rims[:rim], ((0, 0), (0, width + 128)))
    payload = jnp.concatenate([gradients(slice(half, width)).astype(bf16), beside], axis=0)
    got = lax.ppermute(payload, "dom", near_pairs)
    (dpre_late,) = after(payload, dpre)
    term = dot_t(dot(onehot(s_order, edges), dpre_late).astype(bf16), w_edge).astype(bf16)
    section_got = section_send(term, 0)
    from_near = got[half:, :width]
    sums = gradients(slice(0, half)) + got[:half].astype(f32)
    (sums,) = after(term, sums.astype(bf16))

    term, section_got = after(sums, term, section_got)
    sums = lax.all_to_all(sums.reshape(4, half // 4, -1), "dom", 0, 0, axis_index_groups=ALONG_X)
    term = section_add(term, section_got)
    section_got = section_send(term, 1)
    sums = jnp.sum(sums.astype(f32), axis=0).astype(bf16)
    (sums,) = after(term, sums)

    term, section_got, rims, table, up = after(sums, term, section_got, rims, table, up)
    sums = lax.all_to_all(sums.reshape(8, half // 32, -1), "dom", 0, 0, axis_index_groups=ALONG_Z)
    term = section_add(term, section_got)
    section_got = section_send(term, 2)
    from_far = lax.ppermute(rims[rim:], "dom", far_pairs)
    part = own_part(up, table)
    (sums,) = after(term, sums)
    sums = jnp.sum(sums.astype(f32), axis=0)

    node_grads = joined(part, from_near, from_far)
    edge_grad, send_grad, gain_grad = sums[:, :width], sums[:, width : 2 * width], sums[:, 2 * width]
    term = section_add(term, section_got)

    return (
        node_grads[None, None],
        term[None],
        edge_grad[None],
        send_grad[None],
        gain_grad[None],
    )


def solution(mesh):
    return jax.shard_map(
        on_device,
        mesh=mesh,
        in_specs=(
            P("section", None, "dom", None),
            P(None, "dom", None),
            P(None, "dom", None),
            P("section", None, None),
            P("section", None, None),
            P("section", None),
            P("dom"),
            P("dom"),
            P("dom"),
            P("dom"),
        ),
        out_specs=(
            P("section", None, "dom", None),
            P(None, ("dom", "section"), None),
            P("section", "dom", None),
            P("section", "dom", None),
            P("section", "dom"),
        ),
        check_vma=False,
    )
```

```python
import numpy as np
import jax
import jax.numpy as jnp
from jax import lax
from jax.sharding import PartitionSpec as P

EDGE_BLOCK = 128
NORM_EPSILON = 1e-05

ALONG_X = [[z * 8 + x * 2 + c for x in range(4)] for z in range(8) for c in range(2)]
ALONG_Z = [[z * 8 + x * 2 + c for z in range(8)] for x in range(4) for c in range(2)]


def section_order(sections):
    table = np.zeros((sections, sections), np.int32)
    for s in range(sections):
        for j in range(sections):
            table[s, j] = s ^ sum(((j >> (2 - k)) & 1) << k for k in range(3))
    return table


def after(mark, *values):
    return lax.optimization_barrier((mark, *values))[1:]


def onehot(index, count):
    return (index[:, None] == jnp.arange(count, dtype=jnp.int32)[None, :]).astype(jnp.bfloat16)


def onehot_t(index, count):
    return (jnp.arange(count, dtype=jnp.int32)[:, None] == index[None, :]).astype(jnp.bfloat16)


def dot(a, b):
    return jnp.dot(a, b, preferred_element_type=jnp.float32)


def dot_t(a, b):
    return lax.dot_general(a, b, (((1,), (1,)), ((), ())), preferred_element_type=jnp.float32)


def spread(chunks, size):
    return (chunks[:, None] * size + jnp.arange(size, dtype=jnp.int32)[None, :]).reshape(-1)


def on_device(
    node_states,
    edge_features,
    out_cotangent,
    edge_weight,
    send_weight,
    layer_norm_gain,
    edge_sender,
    edge_receiver,
    halo_rows,
    block_counts,
):
    bf16, f32 = jnp.bfloat16, jnp.float32
    h = node_states[0, 0]
    feats = edge_features[0]
    w_edge, w_send, gain = edge_weight[0], send_weight[0], layer_norm_gain[0]
    nodes, width = h.shape
    edges = feats.shape[0]
    rim = halo_rows.shape[0] // 2
    rows = nodes + 2 * rim
    sections, doms = lax.axis_size("section"), lax.axis_size("dom")
    section, dom = lax.axis_index("section"), lax.axis_index("dom")

    near = [p ^ 1 for p in range(doms)]
    far = [(p + 1) % doms if p % 2 else (p - 1) % doms for p in range(doms)]
    near_pairs, far_pairs = list(enumerate(near)), list(enumerate(far))
    even = dom % 2 == 0
    label = jnp.arange(rows, dtype=jnp.int32)
    label = jnp.where(even & (label >= nodes), nodes + (label - nodes + rim) % (2 * rim), label)

    chosen = dot(onehot(halo_rows, nodes), h).astype(bf16)
    from_far = lax.ppermute(jnp.where(even, chosen[:rim], chosen[rim : 2 * rim]), "dom", far_pairs)
    from_near = lax.ppermute(jnp.where(even, chosen[rim : 2 * rim], chosen[:rim]), "dom", near_pairs)
    h_rim = jnp.concatenate([from_near, from_far], axis=0)
    ends = lax.optimization_barrier(jnp.minimum(jnp.concatenate([edge_sender, edge_receiver]), rows - 1))
    edge_sender, edge_receiver = ends[:edges], ends[edges:]
    send_hot = (edge_sender[:, None] == label[None, :]).astype(bf16)
    send_hot_t = (label[:, None] == edge_sender[None, :]).astype(bf16)
    recv_hot = onehot(edge_receiver, nodes)
    recv_hot_t = onehot_t(edge_receiver, nodes)
    live = (jnp.arange(edges, dtype=jnp.int32) // EDGE_BLOCK < block_counts[0]).astype(f32)[:, None]
    own = dot(h, w_send).astype(bf16)
    base = lax.optimization_barrier(dot(feats, w_edge) + dot(send_hot[:, :nodes], own))
    pre = lax.optimization_barrier(base + dot(send_hot[:, nodes:], dot(h_rim, w_send).astype(bf16)))
    sig = jax.nn.sigmoid(pre)
    message = (live * (pre * sig)).astype(bf16)
    slope = live * (sig * (1.0 + pre * (1.0 - sig)))
    slope = lax.optimization_barrier(slope)
    agg = dot(recv_hot_t, message)
    scale = lax.rsqrt(jnp.mean(agg * agg, axis=-1, keepdims=True) + NORM_EPSILON)
    normed = agg * scale

    def backward(up):
        up_wide = up.astype(f32)
        dnorm = up_wide * gain
        dagg = scale * (dnorm - normed * jnp.mean(dnorm * normed, axis=-1, keepdims=True))
        gathered = dot(recv_hot, dagg.astype(bf16))
        dpre = (slope * gathered).astype(bf16)
        return dpre, dot(send_hot_t, dpre).astype(bf16)

    def own_part(up, table):
        return (up.astype(f32) + dot_t(table[:nodes], w_send)).astype(bf16)

    def rim_part(table):
        return dot_t(table[nodes:], w_send).astype(bf16)

    def joined(part, from_near, from_far):
        rims = jnp.concatenate([from_near, from_far], axis=0)
        return (part.astype(f32) + dot(select_t, rims)).astype(bf16)

    def hop(value, t, target):
        top = sections - 1 - t
        pairs = [(top * doms + p, (top - 1) * doms + target[p]) for p in range(doms)]
        return lax.ppermute(value, ("section", "dom"), pairs)

    up = out_cotangent[0]
    held = jnp.where(section == sections - 1, up, jnp.zeros_like(up))
    for t in range(sections - 1):
        _, table = backward(up)
        back = dot_t(table, w_send)
        part, rims = (up.astype(f32) + back[:nodes]).astype(bf16), back[nodes:].astype(bf16)
        if t == 0:
            (rows_late,) = after(part, halo_rows)
            rows_late = jnp.where(even, jnp.concatenate([rows_late[rim:], rows_late[:rim]]), rows_late)
            select_t = onehot_t(rows_late, nodes)
        else:
            held_late, up_late = after(part[:8, :128], held, up)
            held = held_late + up_late
        from_far = hop(rims[rim:], t, far)
        from_near = hop(rims[:rim], t, near)
        up = joined(hop(part, t, range(doms)), from_near, from_far)
        if t == sections - 3:
            feats_late, h_late, h_rim_late, dom_late, section_late = after(
                part[:8, :128], feats, h, h_rim, dom, section
            )
            place = jnp.arange(doms, dtype=jnp.int32)
            chunk = (place % 8) * 8 + (place // 8 % 4) * 2 + (dom_late + place // 32) % 2
            order = spread(chunk, width // doms)
            mixer = onehot(order, width)
            feats_t = dot_t(mixer, feats_late).astype(bf16)
            h_t = jnp.concatenate([dot_t(mixer, h_late), dot_t(mixer, h_rim_late)], axis=1).astype(bf16)
            s_order = lax.dynamic_index_in_dim(jnp.asarray(section_order(sections)), section_late, 0, keepdims=False)
            s_order = spread(s_order, edges // sections)
            up, order, feats_t, h_t, s_order = lax.optimization_barrier((up, order, feats_t, h_t, s_order))

    up = held + up
    dpre, table = backward(up)
    gain_part = jnp.sum(up.astype(f32) * normed, axis=0)

    def section_send(term, k):
        pairs = [(s, s ^ (1 << k)) for s in range(sections)]
        return lax.ppermute(term[term.shape[0] // 2 :], "section", pairs)

    def section_add(term, got):
        return (term[: got.shape[0]].astype(f32) + got.astype(f32)).astype(bf16)

    half = width // 2
    gain_rows = jnp.broadcast_to(gain_part.astype(bf16)[None], (128, width))

    def gradients(at):
        return jnp.concatenate([dot(feats_t[at], dpre), dot(h_t[at], table), dot_t(onehot(order[at], width), gain_rows)], axis=1)

    rims = rim_part(table)
    beside = jnp.pad(rims[:rim], ((0, 0), (0, width + 128)))
    payload = jnp.concatenate([gradients(slice(half, width)).astype(bf16), beside], axis=0)
    got = lax.ppermute(payload, "dom", near_pairs)
    (dpre_late,) = after(payload, dpre)
    at = edges // 2
    term_away = dot_t(dot(onehot(s_order[at:], edges), dpre_late).astype(bf16), w_edge).astype(bf16)
    section_got = lax.ppermute(term_away, "section", [(s, s ^ 1) for s in range(sections)])
    sums = gradients(slice(0, half)) + got[:half].astype(f32)
    (sums,) = after(term_away, sums.astype(bf16))

    dpre_late, section_got, rims, table, up = after(sums, dpre, section_got, rims, table, up)
    term = dot_t(dot(onehot(s_order[:at], edges), dpre_late).astype(bf16), w_edge).astype(bf16)
    sums = lax.all_to_all(sums.reshape(4, half // 4, -1), "dom", 0, 0, axis_index_groups=ALONG_X)
    term = section_add(term, section_got)
    section_got = section_send(term, 1)
    from_far = lax.ppermute(rims[rim:], "dom", far_pairs)
    sums = jnp.sum(sums.astype(f32), axis=0).astype(bf16)
    (sums,) = after(term, sums)

    term, section_got = after(sums, term, section_got)
    sums = lax.all_to_all(sums.reshape(8, half // 32, -1), "dom", 0, 0, axis_index_groups=ALONG_Z)
    term = section_add(term, section_got)
    section_got = section_send(term, 2)
    got, from_far, table, up = after(term, got, from_far, table, up)
    node_grads = joined(own_part(up, table), got[half:, :width], from_far)
    (sums,) = after(term, sums)
    sums = jnp.sum(sums.astype(f32), axis=0)

    term, section_got = after(sums, term, section_got)
    edge_grad, send_grad, gain_grad = sums[:, :width], sums[:, width : 2 * width], sums[:, 2 * width]
    term = section_add(term, section_got)

    return (
        node_grads[None, None],
        term[None],
        edge_grad[None],
        send_grad[None],
        gain_grad[None],
    )


def solution(mesh):
    return jax.shard_map(
        on_device,
        mesh=mesh,
        in_specs=(
            P("section", None, "dom", None),
            P(None, "dom", None),
            P(None, "dom", None),
            P("section", None, None),
            P("section", None, None),
            P("section", None),
            P("dom"),
            P("dom"),
            P("dom"),
            P("dom"),
        ),
        out_specs=(
            P("section", None, "dom", None),
            P(None, ("dom", "section"), None),
            P("section", "dom", None),
            P("section", "dom", None),
            P("section", "dom"),
        ),
        check_vma=False,
    )
```

```python
import numpy as np
import jax
import jax.numpy as jnp
from jax import lax
from jax.sharding import PartitionSpec as P

EDGE_BLOCK = 128
NORM_EPSILON = 1e-05

ALONG_X = [[z * 8 + x * 2 + c for x in range(4)] for z in range(8) for c in range(2)]
ALONG_Z = [[z * 8 + x * 2 + c for z in range(8)] for x in range(4) for c in range(2)]


def section_order(sections):
    table = np.zeros((sections, sections), np.int32)
    for s in range(sections):
        for j in range(sections):
            table[s, j] = s ^ sum(((j >> (2 - k)) & 1) << k for k in range(3))
    return table


def after(mark, *values):
    return lax.optimization_barrier((mark, *values))[1:]


def onehot(index, count):
    return (index[:, None] == jnp.arange(count, dtype=jnp.int32)[None, :]).astype(jnp.bfloat16)


def onehot_t(index, count):
    return (jnp.arange(count, dtype=jnp.int32)[:, None] == index[None, :]).astype(jnp.bfloat16)


def dot(a, b):
    return jnp.dot(a, b, preferred_element_type=jnp.float32)


def dot_t(a, b):
    return lax.dot_general(a, b, (((1,), (1,)), ((), ())), preferred_element_type=jnp.float32)


def spread(chunks, size):
    return (chunks[:, None] * size + jnp.arange(size, dtype=jnp.int32)[None, :]).reshape(-1)


def on_device(
    node_states,
    edge_features,
    out_cotangent,
    edge_weight,
    send_weight,
    layer_norm_gain,
    edge_sender,
    edge_receiver,
    halo_rows,
    block_counts,
):
    bf16, f32 = jnp.bfloat16, jnp.float32
    h = node_states[0, 0]
    feats = edge_features[0]
    w_edge, w_send, gain = edge_weight[0], send_weight[0], layer_norm_gain[0]
    nodes, width = h.shape
    edges = feats.shape[0]
    rim = halo_rows.shape[0] // 2
    rows = nodes + 2 * rim
    sections, doms = lax.axis_size("section"), lax.axis_size("dom")
    section, dom = lax.axis_index("section"), lax.axis_index("dom")

    near = [p ^ 1 for p in range(doms)]
    far = [(p + 1) % doms if p % 2 else (p - 1) % doms for p in range(doms)]
    near_pairs, far_pairs = list(enumerate(near)), list(enumerate(far))
    even = dom % 2 == 0
    label = jnp.arange(rows, dtype=jnp.int32)
    label = jnp.where(even & (label >= nodes), nodes + (label - nodes + rim) % (2 * rim), label)

    chosen = dot(onehot(halo_rows, nodes), h).astype(bf16)
    from_far = lax.ppermute(jnp.where(even, chosen[:rim], chosen[rim : 2 * rim]), "dom", far_pairs)
    from_near = lax.ppermute(jnp.where(even, chosen[rim : 2 * rim], chosen[:rim]), "dom", near_pairs)
    h_rim = jnp.concatenate([from_near, from_far], axis=0)
    ends = lax.optimization_barrier(jnp.minimum(jnp.concatenate([edge_sender, edge_receiver]), rows - 1))
    edge_sender, edge_receiver = ends[:edges], ends[edges:]
    send_hot = (edge_sender[:, None] == label[None, :]).astype(bf16)
    send_hot_t = (label[:, None] == edge_sender[None, :]).astype(bf16)
    recv_hot = onehot(edge_receiver, nodes)
    recv_hot_t = onehot_t(edge_receiver, nodes)
    live = (jnp.arange(edges, dtype=jnp.int32) // EDGE_BLOCK < block_counts[0]).astype(f32)[:, None]
    own = dot(h, w_send).astype(bf16)
    base = lax.optimization_barrier(dot(feats, w_edge) + dot(send_hot[:, :nodes], own))
    pre = lax.optimization_barrier(base + dot(send_hot[:, nodes:], dot(h_rim, w_send).astype(bf16)))
    sig = jax.nn.sigmoid(pre)
    message = (live * (pre * sig)).astype(bf16)
    slope = live * (sig * (1.0 + pre * (1.0 - sig)))
    slope = lax.optimization_barrier(slope)
    agg = dot(recv_hot_t, message)
    scale = lax.rsqrt(jnp.mean(agg * agg, axis=-1, keepdims=True) + NORM_EPSILON)
    normed = agg * scale

    def backward(up):
        up_wide = up.astype(f32)
        dnorm = up_wide * gain
        dagg = scale * (dnorm - normed * jnp.mean(dnorm * normed, axis=-1, keepdims=True))
        gathered = dot(recv_hot, dagg.astype(bf16))
        dpre = (slope * gathered).astype(bf16)
        return dpre, dot(send_hot_t, dpre).astype(bf16)

    def own_part(up, table):
        return (up.astype(f32) + dot_t(table[:nodes], w_send)).astype(bf16)

    def rim_part(table):
        return dot_t(table[nodes:], w_send).astype(bf16)

    def joined(part, from_near, from_far):
        rims = jnp.concatenate([from_near, from_far], axis=0)
        return (part.astype(f32) + dot(select_t, rims)).astype(bf16)

    def hop(value, t, target):
        top = sections - 1 - t
        pairs = [(top * doms + p, (top - 1) * doms + target[p]) for p in range(doms)]
        return lax.ppermute(value, ("section", "dom"), pairs)

    up = out_cotangent[0]
    held = jnp.where(section == sections - 1, up, jnp.zeros_like(up))
    for t in range(sections - 1):
        _, table = backward(up)
        back = dot_t(table, w_send)
        part, rims = (up.astype(f32) + back[:nodes]).astype(bf16), back[nodes:].astype(bf16)
        if t == 0:
            (rows_late,) = after(part, halo_rows)
            rows_late = jnp.where(even, jnp.concatenate([rows_late[rim:], rows_late[:rim]]), rows_late)
            select_t = onehot_t(rows_late, nodes)
        elif t == 1:
            held_late, up_late = after(part[:8, :128], held, up)
            held = held_late + up_late
        elif t % 2:
            held_late, before_late, up_late = after(part[:8, :128], held, before, up)
            held = held_late + (before_late + up_late)
        elif t == sections - 2:
            held_late, up_late = after(part[:8, :128], held, up)
            held = held_late + up_late
        before = up
        from_far = hop(rims[rim:], t, far)
        from_near = hop(rims[:rim], t, near)
        up = joined(hop(part, t, range(doms)), from_near, from_far)
        if t == sections - 3:
            feats_late, h_late, h_rim_late, dom_late, section_late = after(
                part[:8, :128], feats, h, h_rim, dom, section
            )
            place = jnp.arange(doms, dtype=jnp.int32)
            chunk = (place % 8) * 8 + (place // 8 % 4) * 2 + (dom_late + place // 32) % 2
            order = spread(chunk, width // doms)
            mixer = onehot(order, width)
            feats_t = dot_t(mixer, feats_late).astype(bf16)
            h_t = jnp.concatenate([dot_t(mixer, h_late), dot_t(mixer, h_rim_late)], axis=1).astype(bf16)
            s_order = lax.dynamic_index_in_dim(jnp.asarray(section_order(sections)), section_late, 0, keepdims=False)
            s_order = spread(s_order, edges // sections)
            up, order, feats_t, h_t, s_order = lax.optimization_barrier((up, order, feats_t, h_t, s_order))

    up = held + up
    dpre, table = backward(up)
    gain_part = jnp.sum(up.astype(f32) * normed, axis=0)

    def section_send(term, k):
        pairs = [(s, s ^ (1 << k)) for s in range(sections)]
        return lax.ppermute(term[term.shape[0] // 2 :], "section", pairs)

    def section_add(term, got):
        return (term[: got.shape[0]].astype(f32) + got.astype(f32)).astype(bf16)

    half = width // 2
    gain_rows = jnp.broadcast_to(gain_part.astype(bf16)[None], (128, width))

    def gradients(at):
        return jnp.concatenate([dot(feats_t[at], dpre), dot(h_t[at], table), dot_t(onehot(order[at], width), gain_rows)], axis=1)

    rims = rim_part(table)
    beside = jnp.pad(rims[:rim], ((0, 0), (0, width + 128)))
    payload = jnp.concatenate([gradients(slice(half, width)).astype(bf16), beside], axis=0)
    got = lax.ppermute(payload, "dom", near_pairs)
    (dpre_late,) = after(payload, dpre)
    at = edges // 2
    term_away = dot_t(dot(onehot(s_order[at:], edges), dpre_late).astype(bf16), w_edge).astype(bf16)
    section_got = lax.ppermute(term_away, "section", [(s, s ^ 1) for s in range(sections)])
    sums = gradients(slice(0, half)) + got[:half].astype(f32)
    (sums,) = after(term_away, sums.astype(bf16))

    dpre_late, section_got, rims, table, up = after(sums, dpre, section_got, rims, table, up)
    term = dot_t(dot(onehot(s_order[:at], edges), dpre_late).astype(bf16), w_edge).astype(bf16)
    sums = lax.all_to_all(sums.reshape(4, half // 4, -1), "dom", 0, 0, axis_index_groups=ALONG_X)
    term = section_add(term, section_got)
    section_got = section_send(term, 1)
    from_far = lax.ppermute(rims[rim:], "dom", far_pairs)
    sums = jnp.sum(sums.astype(f32), axis=0).astype(bf16)
    (sums,) = after(term, sums)

    term, section_got = after(sums, term, section_got)
    sums = lax.all_to_all(sums.reshape(8, half // 32, -1), "dom", 0, 0, axis_index_groups=ALONG_Z)
    term = section_add(term, section_got)
    section_got = section_send(term, 2)
    got, from_far, table, up = after(term, got, from_far, table, up)
    node_grads = joined(own_part(up, table), got[half:, :width], from_far)
    (sums,) = after(term, sums)
    sums = jnp.sum(sums.astype(f32), axis=0)

    term, section_got = after(sums, term, section_got)
    edge_grad, send_grad, gain_grad = sums[:, :width], sums[:, width : 2 * width], sums[:, 2 * width]
    term = section_add(term, section_got)

    return (
        node_grads[None, None],
        term[None],
        edge_grad[None],
        send_grad[None],
        gain_grad[None],
    )


def solution(mesh):
    return jax.shard_map(
        on_device,
        mesh=mesh,
        in_specs=(
            P("section", None, "dom", None),
            P(None, "dom", None),
            P(None, "dom", None),
            P("section", None, None),
            P("section", None, None),
            P("section", None),
            P("dom"),
            P("dom"),
            P("dom"),
            P("dom"),
        ),
        out_specs=(
            P("section", None, "dom", None),
            P(None, ("dom", "section"), None),
            P("section", "dom", None),
            P("section", "dom", None),
            P("section", "dom"),
        ),
        check_vma=False,
    )
```

```python
import numpy as np
import jax
import jax.numpy as jnp
from jax import lax
from jax.sharding import PartitionSpec as P

EDGE_BLOCK = 128
NORM_EPSILON = 1e-05

ALONG_X = [[z * 8 + x * 2 + c for x in range(4)] for z in range(8) for c in range(2)]
ALONG_Z = [[z * 8 + x * 2 + c for z in range(8)] for x in range(4) for c in range(2)]


def section_order(sections):
    table = np.zeros((sections, sections), np.int32)
    for s in range(sections):
        for j in range(sections):
            table[s, j] = s ^ sum(((j >> (2 - k)) & 1) << k for k in range(3))
    return table


def after(mark, *values):
    return lax.optimization_barrier((mark, *values))[1:]


def onehot(index, count):
    return (index[:, None] == jnp.arange(count, dtype=jnp.int32)[None, :]).astype(jnp.bfloat16)


def onehot_t(index, count):
    return (jnp.arange(count, dtype=jnp.int32)[:, None] == index[None, :]).astype(jnp.bfloat16)


def dot(a, b):
    return jnp.dot(a, b, preferred_element_type=jnp.float32)


def dot_t(a, b):
    return lax.dot_general(a, b, (((1,), (1,)), ((), ())), preferred_element_type=jnp.float32)


def spread(chunks, size):
    return (chunks[:, None] * size + jnp.arange(size, dtype=jnp.int32)[None, :]).reshape(-1)


def on_device(
    node_states,
    edge_features,
    out_cotangent,
    edge_weight,
    send_weight,
    layer_norm_gain,
    edge_sender,
    edge_receiver,
    halo_rows,
    block_counts,
):
    bf16, f32 = jnp.bfloat16, jnp.float32
    h = node_states[0, 0]
    feats = edge_features[0]
    w_edge, w_send, gain = edge_weight[0], send_weight[0], layer_norm_gain[0]
    nodes, width = h.shape
    edges = feats.shape[0]
    rim = halo_rows.shape[0] // 2
    rows = nodes + 2 * rim
    sections, doms = lax.axis_size("section"), lax.axis_size("dom")
    section, dom = lax.axis_index("section"), lax.axis_index("dom")

    near = [p ^ 1 for p in range(doms)]
    far = [(p + 1) % doms if p % 2 else (p - 1) % doms for p in range(doms)]
    near_pairs, far_pairs = list(enumerate(near)), list(enumerate(far))
    even = dom % 2 == 0
    label = jnp.arange(rows, dtype=jnp.int32)
    label = jnp.where(even & (label >= nodes), nodes + (label - nodes + rim) % (2 * rim), label)

    chosen = dot(onehot(halo_rows, nodes), h).astype(bf16)
    from_far = lax.ppermute(jnp.where(even, chosen[:rim], chosen[rim : 2 * rim]), "dom", far_pairs)
    from_near = lax.ppermute(jnp.where(even, chosen[rim : 2 * rim], chosen[:rim]), "dom", near_pairs)
    h_rim = jnp.concatenate([from_near, from_far], axis=0)
    ends = lax.optimization_barrier(jnp.minimum(jnp.concatenate([edge_sender, edge_receiver]), rows - 1))
    edge_sender, edge_receiver = ends[:edges], ends[edges:]
    ends = lax.optimization_barrier(jnp.minimum(jnp.concatenate([edge_sender, edge_receiver]), rows - 1))
    edge_sender, edge_receiver = ends[:edges], ends[edges:]
    send_hot = (edge_sender[:, None] == label[None, :]).astype(bf16)
    send_hot_t = (label[:, None] == edge_sender[None, :]).astype(bf16)
    recv_hot = onehot(edge_receiver, nodes)
    recv_hot_t = onehot_t(edge_receiver, nodes)
    live = (jnp.arange(edges, dtype=jnp.int32) // EDGE_BLOCK < block_counts[0]).astype(f32)[:, None]
    own = dot(h, w_send).astype(bf16)
    base = lax.optimization_barrier(dot(feats, w_edge) + dot(send_hot[:, :nodes], own))
    pre = lax.optimization_barrier(base + dot(send_hot[:, nodes:], dot(h_rim, w_send).astype(bf16)))
    sig = jax.nn.sigmoid(pre)
    message = (live * (pre * sig)).astype(bf16)
    slope = live * (sig * (1.0 + pre * (1.0 - sig)))
    slope = lax.optimization_barrier(slope)
    agg = dot(recv_hot_t, message)
    scale = lax.rsqrt(jnp.mean(agg * agg, axis=-1, keepdims=True) + NORM_EPSILON)
    normed = agg * scale

    def backward(up):
        up_wide = up.astype(f32)
        dnorm = up_wide * gain
        dagg = scale * (dnorm - normed * jnp.mean(dnorm * normed, axis=-1, keepdims=True))
        gathered = dot(recv_hot, dagg.astype(bf16))
        dpre = (slope * gathered).astype(bf16)
        return dpre, dot(send_hot_t, dpre).astype(bf16)

    def own_part(up, table):
        return (up.astype(f32) + dot_t(table[:nodes], w_send)).astype(bf16)

    def rim_part(table):
        return dot_t(table[nodes:], w_send).astype(bf16)

    def joined(part, from_near, from_far):
        rims = jnp.concatenate([from_near, from_far], axis=0)
        return (part.astype(f32) + dot(select_t, rims)).astype(bf16)

    def hop(value, t, target):
        top = sections - 1 - t
        pairs = [(top * doms + p, (top - 1) * doms + target[p]) for p in range(doms)]
        return lax.ppermute(value, ("section", "dom"), pairs)

    up = out_cotangent[0]
    held = jnp.where(section == sections - 1, up, jnp.zeros_like(up))
    for t in range(sections - 1):
        _, table = backward(up)
        back = dot_t(table, w_send)
        part, rims = (up.astype(f32) + back[:nodes]).astype(bf16), back[nodes:].astype(bf16)
        if t == 0:
            (rows_late,) = after(part, halo_rows)
            rows_late = jnp.where(even, jnp.concatenate([rows_late[rim:], rows_late[:rim]]), rows_late)
            select_t = onehot_t(rows_late, nodes)
        elif t == 1:
            held_late, up_late = after(part[:8, :128], held, up)
            held = held_late + up_late
        elif t % 2:
            held_late, before_late, up_late = after(part[:8, :128], held, before, up)
            held = held_late + (before_late + up_late)
        elif t == sections - 2:
            held_late, up_late = after(part[:8, :128], held, up)
            held = held_late + up_late
        before = up
        from_far = hop(rims[rim:], t, far)
        from_near = hop(rims[:rim], t, near)
        up = joined(hop(part, t, range(doms)), from_near, from_far)
        if t == sections - 3:
            feats_late, h_late, h_rim_late, dom_late, section_late = after(
                part[:8, :128], feats, h, h_rim, dom, section
            )
            place = jnp.arange(doms, dtype=jnp.int32)
            chunk = (place % 8) * 8 + (place // 8 % 4) * 2 + (dom_late + place // 32) % 2
            order = spread(chunk, width // doms)
            mixer = onehot(order, width)
            feats_t = dot_t(mixer, feats_late).astype(bf16)
            h_t = jnp.concatenate([dot_t(mixer, h_late), dot_t(mixer, h_rim_late)], axis=1).astype(bf16)
            s_order = lax.dynamic_index_in_dim(jnp.asarray(section_order(sections)), section_late, 0, keepdims=False)
            s_order = spread(s_order, edges // sections)
            up, order, feats_t, h_t, s_order = lax.optimization_barrier((up, order, feats_t, h_t, s_order))

    up = held + up
    dpre, table = backward(up)
    gain_part = jnp.sum(up.astype(f32) * normed, axis=0)

    def section_send(term, k):
        pairs = [(s, s ^ (1 << k)) for s in range(sections)]
        return lax.ppermute(term[term.shape[0] // 2 :], "section", pairs)

    def section_add(term, got):
        return (term[: got.shape[0]].astype(f32) + got.astype(f32)).astype(bf16)

    half = width // 2
    gain_rows = jnp.broadcast_to(gain_part.astype(bf16)[None], (128, width))

    def gradients(at):
        return jnp.concatenate([dot(feats_t[at], dpre), dot(h_t[at], table), dot_t(onehot(order[at], width), gain_rows)], axis=1)

    rims = rim_part(table)
    beside = jnp.pad(rims[:rim], ((0, 0), (0, width + 128)))
    payload = jnp.concatenate([gradients(slice(half, width)).astype(bf16), beside], axis=0)
    got = lax.ppermute(payload, "dom", near_pairs)
    (dpre_late,) = after(payload, dpre)
    at = edges // 2
    term_away = dot_t(dot(onehot(s_order[at:], edges), dpre_late).astype(bf16), w_edge).astype(bf16)
    section_got = lax.ppermute(term_away, "section", [(s, s ^ 1) for s in range(sections)])
    sums = gradients(slice(0, half)) + got[:half].astype(f32)
    (sums,) = after(term_away, sums.astype(bf16))

    dpre_late, section_got, rims, table, up = after(sums, dpre, section_got, rims, table, up)
    term = dot_t(dot(onehot(s_order[:at], edges), dpre_late).astype(bf16), w_edge).astype(bf16)
    sums = lax.all_to_all(sums.reshape(4, half // 4, -1), "dom", 0, 0, axis_index_groups=ALONG_X)
    term = section_add(term, section_got)
    section_got = section_send(term, 1)
    from_far = lax.ppermute(rims[rim:], "dom", far_pairs)
    sums = jnp.sum(sums.astype(f32), axis=0).astype(bf16)
    (sums,) = after(term, sums)

    term, section_got = after(sums, term, section_got)
    sums = lax.all_to_all(sums.reshape(8, half // 32, -1), "dom", 0, 0, axis_index_groups=ALONG_Z)
    term = section_add(term, section_got)
    section_got = section_send(term, 2)
    got, from_far, table, up = after(term, got, from_far, table, up)
    node_grads = joined(own_part(up, table), got[half:, :width], from_far)
    (sums,) = after(term, sums)
    sums = jnp.sum(sums.astype(f32), axis=0)

    term, section_got = after(sums, term, section_got)
    edge_grad, send_grad, gain_grad = sums[:, :width], sums[:, width : 2 * width], sums[:, 2 * width]
    term = section_add(term, section_got)

    return (
        node_grads[None, None],
        term[None],
        edge_grad[None],
        send_grad[None],
        gain_grad[None],
    )


def solution(mesh):
    return jax.shard_map(
        on_device,
        mesh=mesh,
        in_specs=(
            P("section", None, "dom", None),
            P(None, "dom", None),
            P(None, "dom", None),
            P("section", None, None),
            P("section", None, None),
            P("section", None),
            P("dom"),
            P("dom"),
            P("dom"),
            P("dom"),
        ),
        out_specs=(
            P("section", None, "dom", None),
            P(None, ("dom", "section"), None),
            P("section", "dom", None),
            P("section", "dom", None),
            P("section", "dom"),
        ),
        check_vma=False,
    )
```
